32 devices in a mesh: groups: 2 (over y), rows: 8 (over z, x), cols: 2 (over core).
Axes of the slice: x: 2, y: 2, z: 4, core: 2. Of those that a mesh axis runs over, the one named last changes fastest.
Arguments:
- plume_field: bfloat16 [64, 64, 1024], P(None, ('groups', 'rows'), 'cols'), parts along dimension 1, may hold values from -6 to 6
- spectral_weight: bfloat16 [2, 1024, 64, 128], P(None, ('rows', 'cols')), may hold values from -0.5 to 0.5
- point_weight: bfloat16 [2, 64, 64], replicated, may hold values from -0.75 to 0.75
- conv_weight: bfloat16 [2, 3, 64, 64, 3, 3], replicated, may hold values from -0.25 to 0.25
Outputs:
- layer_output: bfloat16 [64, 64, 1024], P(None, ('groups', 'rows'), 'cols'), parts along dimension 1
The draws below stay inside these ranges and needn't reach their ends.
There are 2 independent parts, one for each index of `groups`. The reference program is written for one: setup_inputs(seed, part) draws one part's arguments, and reference() takes and returns one part's arrays. A program takes and returns all parts, laid end to end along the dimension named above; an argument that names none is the same for every part. Nothing has to cross between parts.
All inputs are finite; a program needn't handle non-finite values.
Results may differ from the reference program's by a relative error of at most 0.015.
Values may be sent and summed in bfloat16 or wider, within the bound.
A program may use at most 64 MiB of HBM per device.

```python
import math
import jax
import jax.numpy as jnp
from jax import lax

CH = 64
MR = 32
MC = 32
LAYERS = 2
NROWS = 32
NCOLS = 1024
MODES = 1024


def steps_of(rng, dims, cuts, smallest, largest):
    loudness = 1.0
    for axis_at, parts in cuts:
        heights = jax.random.uniform(jax.random.fold_in(jax.random.fold_in(rng, 6), axis_at), (parts,), jnp.float32, smallest / len(cuts), largest / len(cuts))
        loudness = loudness * jnp.repeat(jnp.exp(heights), dims[axis_at] // parts).reshape((-1,) + (1,) * (len(dims) - 1 - axis_at))
    return loudness


def normal_values(rng, shape, width, bound, shards=(), held_as=jnp.bfloat16):
    values = width * jax.random.normal(rng, shape, jnp.float32)
    if shards:
        values = values * steps_of(rng, shape, shards, -0.22, 0.18)
    return jnp.clip(values, -bound, bound).astype(held_as)


def setup_inputs(seed: int = 0, part: int = 0) -> dict:
    streams_of = jax.random.split(jax.random.key(seed), 5)
    own_keys = jax.random.split(jax.random.fold_in(streams_of[4], part), 5)
    plume_field = normal_values(own_keys[0], (CH, NROWS, NCOLS), 1.0, 6.0, ((1, 8), (2, 2)))
    spectral_weight = normal_values(streams_of[1], (LAYERS, MODES, CH, 2 * CH), (2 * CH) ** -0.5, 0.5, ((1, 16),))
    point_weight = normal_values(streams_of[2], (LAYERS, CH, CH), CH ** -0.5, 0.75)
    conv_weight = normal_values(streams_of[3], (LAYERS, 3, CH, CH, 3, 3), (9 * CH) ** -0.5, 0.25)
    return dict(plume_field=plume_field, spectral_weight=spectral_weight, point_weight=point_weight, conv_weight=conv_weight)


def angles(frequencies, positions, extent):
    product = frequencies[:, None] * positions[None, :] % extent
    return 2.0 * math.pi / extent * product.astype(jnp.float32)

def row_frequencies(extent):
    wave_index = jnp.arange(MR, dtype=jnp.int32)
    return jnp.where(wave_index < MR // 2, wave_index, extent - MR + wave_index).astype(jnp.int32)

def contract(form, left, right):
    return jnp.einsum(form, left, right, precision=lax.Precision.HIGHEST)

def spectral_branch(plume_field, weight):
    row_count, col_count = (plume_field.shape[1], plume_field.shape[2])
    row_theta = angles(row_frequencies(row_count), jnp.arange(row_count, dtype=jnp.int32), row_count)
    col_theta = angles(jnp.arange(MC, dtype=jnp.int32), jnp.arange(col_count, dtype=jnp.int32), col_count)
    cos_rows, sin_rows = (jnp.cos(row_theta), jnp.sin(row_theta))
    forward_table = jnp.concatenate([jnp.cos(col_theta), jnp.sin(col_theta)], 0).T.astype(jnp.bfloat16)
    partial_value = contract('cxy,yk->cxk', plume_field.astype(jnp.float32), forward_table.astype(jnp.float32))
    part_re, part_im = (partial_value[..., :MC], -partial_value[..., MC:])
    four_re = contract('kx,cxj->kjc', cos_rows, part_re) + contract('kx,cxj->kjc', sin_rows, part_im)
    four_im = contract('kx,cxj->kjc', cos_rows, part_im) - contract('kx,cxj->kjc', sin_rows, part_re)
    spectrum = jnp.concatenate([four_re, four_im], -1).reshape(MR * MC, 2 * CH) / math.sqrt(row_count * col_count)
    rounded = lax.optimization_barrier(spectrum.astype(jnp.bfloat16)).astype(jnp.float32)
    weight_wide = weight.astype(jnp.float32)
    from_re = contract('mc,mcd->md', rounded[:, :CH], weight_wide)
    from_im = contract('mc,mcd->md', rounded[:, CH:], weight_wide)
    mixed_modes = jnp.concatenate([from_re[:, :CH] - from_im[:, CH:], from_re[:, CH:] + from_im[:, :CH]], -1)
    mixed_modes = lax.optimization_barrier(mixed_modes.astype(jnp.bfloat16)).astype(jnp.float32)
    mixed_modes = mixed_modes.reshape(MR, MC, 2 * CH)
    mode_re, mode_im = (mixed_modes[..., :CH], mixed_modes[..., CH:])
    back_re = contract('kx,kjc->jxc', cos_rows, mode_re) - contract('kx,kjc->jxc', sin_rows, mode_im)
    back_im = contract('kx,kjc->jxc', sin_rows, mode_re) + contract('kx,kjc->jxc', cos_rows, mode_im)
    back_table = jnp.concatenate([jnp.cos(col_theta), -jnp.sin(col_theta)], 0)
    stacked = jnp.concatenate([back_re, back_im], 0)
    return contract('jxc,jy->cxy', stacked, back_table) / math.sqrt(MR * MC)

def convolve(values, kernel):
    result = lax.conv_general_dilated(values[None].astype(jnp.float32), kernel.astype(jnp.float32), (1, 1), ((1, 1), (1, 1)), dimension_numbers=('NCHW', 'OIHW', 'NCHW'), precision=lax.Precision.HIGHEST)
    return result[0]

def reference(plume_field, spectral_weight, point_weight, conv_weight):
    for layer_index in range(LAYERS):
        spectral_part = spectral_branch(plume_field, spectral_weight[layer_index])
        point_part = contract('co,cxy->oxy', point_weight[layer_index].astype(jnp.float32), plume_field.astype(jnp.float32))
        first = jax.nn.gelu(convolve(plume_field, conv_weight[layer_index, 0])).astype(jnp.bfloat16)
        second = jax.nn.gelu(convolve(first, conv_weight[layer_index, 1])).astype(jnp.bfloat16)
        summed = spectral_part + point_part + convolve(second, conv_weight[layer_index, 2])
        plume_field = jax.nn.gelu(summed).astype(jnp.bfloat16)
    return plume_field
```

```python
import math

import functools

import jax
import jax.numpy as jnp
import numpy as np
from jax import lax
from jax.experimental import pallas as pl
from jax.experimental.pallas import tpu as pltpu
from jax.sharding import PartitionSpec as P

CH = 64
MR = 32
MC = 32
LAYERS = 2


def with_halo(cells, sides, width):
    for axis, dim in sides:
        count = lax.axis_size(axis)
        ends = count - 1
        head = lax.slice_in_dim(cells, 0, width, axis=dim)
        tail = lax.slice_in_dim(cells, cells.shape[dim] - width, cells.shape[dim], axis=dim)
        cells = jnp.concatenate(
            [
                lax.ppermute(tail, axis, [(i, (i + 1) % count) for i in range(ends)]),
                cells,
                lax.ppermute(head, axis, [((i + 1) % count, i) for i in range(ends)]),
            ],
            axis=dim,
        )
    return cells


def angles(frequencies, positions, extent):
    product = frequencies[:, None] * positions[None, :] % extent
    return 2.0 * math.pi / extent * product.astype(jnp.float32)


def row_frequencies(extent):
    wave_index = jnp.arange(MR, dtype=jnp.int32)
    return jnp.where(wave_index < MR // 2, wave_index, extent - MR + wave_index)


def contract(form, left, right):
    return jnp.einsum(form, left, right, precision=lax.Precision.HIGHEST)


def convolve_valid(padded, kernel):
    result = lax.conv_general_dilated(
        padded[None],
        kernel,
        (1, 1),
        "VALID",
        dimension_numbers=("NCHW", "OIHW", "NCHW"),
        preferred_element_type=jnp.float32,
    )
    return result[0]


def rim_once(values):
    return with_halo(values, (("rows", 1), ("cols", 2)), 1)


def shards(plume_field, spectral_weight, point_weight, conv_weight):
    rows_here, cols_here = (plume_field.shape[1], plume_field.shape[2])
    row_devices, col_devices = (lax.axis_size("rows"), lax.axis_size("cols"))
    row_count, col_count = (rows_here * row_devices, cols_here * col_devices)
    row_start = lax.axis_index("rows") * rows_here
    col_start = lax.axis_index("cols") * cols_here
    row_positions = row_start + jnp.arange(rows_here, dtype=jnp.int32)
    col_positions = col_start + jnp.arange(cols_here, dtype=jnp.int32)
    row_theta = angles(row_frequencies(row_count), row_positions, row_count)
    col_theta = angles(jnp.arange(MC, dtype=jnp.int32), col_positions, col_count)
    cos_rows, sin_rows = (jnp.cos(row_theta), jnp.sin(row_theta))
    all_theta = angles(
        row_frequencies(row_count), jnp.arange(row_count, dtype=jnp.int32), row_count
    )
    cos_every, sin_every = (jnp.cos(all_theta), jnp.sin(all_theta))
    forward_table = jnp.concatenate([jnp.cos(col_theta), jnp.sin(col_theta)], 0).T.astype(
        jnp.bfloat16
    )
    back_table = jnp.concatenate([jnp.cos(col_theta), -jnp.sin(col_theta)], 0)
    norm_factor = 1.0 / math.sqrt(row_count * col_count)
    owned_count = MR * MC // (row_devices * col_devices)
    block_count = MR * MC // row_devices
    block_width = min(block_count, MC)
    block_depth = max(block_count // MC, 1)
    spread = MC // block_width
    pairs_here = block_width * CH // row_devices
    for layer_index in range(LAYERS):
        partial_value = jnp.einsum(
            "cxy,yk->cxk", plume_field, forward_table, preferred_element_type=jnp.float32
        )
        banded = lax.psum(partial_value.astype(jnp.bfloat16), "cols").astype(jnp.float32)
        pencil = banded.reshape(CH, rows_here, 2, spread, block_width).transpose(4, 0, 2, 3, 1)
        pencil = pencil.reshape(block_width * CH, 2, spread, rows_here)
        columns = lax.all_to_all(
            pencil.astype(jnp.bfloat16), "rows", split_axis=0, concat_axis=3, tiled=True
        ).astype(pencil.dtype)
        part_re, part_im = (columns[:, 0], -columns[:, 1])
        four_re = contract("kx,qvx->qvk", cos_every, part_re) + contract(
            "kx,qvx->qvk", sin_every, part_im
        )
        four_im = contract("kx,qvx->qvk", cos_every, part_im) - contract(
            "kx,qvx->qvk", sin_every, part_re
        )
        pencil_spec = jnp.stack([four_re, four_im], 1) * norm_factor
        outgoing = pencil_spec.reshape(
            pairs_here, 2, spread, MR // block_depth, block_depth
        ).transpose(3, 2, 0, 1, 4)
        outgoing = outgoing.reshape(row_devices, pairs_here, 2, block_depth)
        arrived = lax.all_to_all(outgoing, "rows", split_axis=0, concat_axis=0, tiled=True)
        block_spec = (
            arrived.reshape(block_width, CH, 2, block_depth)
            .transpose(3, 0, 2, 1)
            .reshape(block_count, 2 * CH)
        )
        owned_spectrum = lax.dynamic_slice_in_dim(
            block_spec, lax.axis_index("cols") * owned_count, owned_count, 0
        )
        rounded = owned_spectrum.astype(jnp.bfloat16).astype(jnp.float32)
        weight_wide = spectral_weight[layer_index].astype(jnp.float32)
        from_re = contract("mc,mcd->md", rounded[:, :CH], weight_wide)
        from_im = contract("mc,mcd->md", rounded[:, CH:], weight_wide)
        owned_mixed = jnp.concatenate(
            [from_re[:, :CH] - from_im[:, CH:], from_re[:, CH:] + from_im[:, :CH]], -1
        ).astype(jnp.bfloat16)
        every_mode = lax.all_gather(owned_mixed, ("rows", "cols"), axis=0, tiled=True)
        every_mode = every_mode.astype(jnp.float32).reshape(MR, MC, 2 * CH)
        mode_re, mode_im = (every_mode[..., :CH], every_mode[..., CH:])
        back_re = contract("kx,kjc->jxc", cos_rows, mode_re) - contract(
            "kx,kjc->jxc", sin_rows, mode_im
        )
        back_im = contract("kx,kjc->jxc", sin_rows, mode_re) + contract(
            "kx,kjc->jxc", cos_rows, mode_im
        )
        stacked = jnp.concatenate([back_re, back_im], 0)
        spectral_part = contract("jxc,jy->cxy", stacked, back_table) / math.sqrt(MR * MC)
        point_part = jnp.einsum(
            "co,cxy->oxy",
            point_weight[layer_index],
            plume_field,
            preferred_element_type=jnp.float32,
        )
        kernels = conv_weight[layer_index]
        first = jax.nn.gelu(convolve_valid(rim_once(plume_field), kernels[0])).astype(jnp.bfloat16)
        second = jax.nn.gelu(convolve_valid(rim_once(first), kernels[1])).astype(jnp.bfloat16)
        branch_out = convolve_valid(rim_once(second), kernels[2])
        plume_field = jax.nn.gelu(spectral_part + point_part + branch_out).astype(jnp.bfloat16)
    return plume_field


HALO = 3
PAD = 128


def gelu(z):
    return 0.5 * z * (1.0 + jnp.tanh(math.sqrt(2.0 / math.pi) * (z + 0.044715 * z * z * z)))


def dot(a, b):
    return jnp.dot(a, b, preferred_element_type=jnp.float32)


def tables(row_count, col_count, col_devices):
    k = np.arange(MR)
    f1 = np.where(k < MR // 2, k, row_count - MR + k)
    row = 2.0 * math.pi / row_count * (f1[:, None] * np.arange(row_count)[None] % row_count)
    col = 2.0 * math.pi / col_count * (np.arange(MC)[:, None] * np.arange(col_count)[None] % col_count)
    split = lambda t: t.reshape(2 * MC, col_devices, -1).transpose(1, 0, 2)
    fwd = split(np.concatenate([np.cos(col), np.sin(col)], 0)).astype(jnp.bfloat16)
    back = split(np.concatenate([np.cos(col), -np.sin(col)], 0) / math.sqrt(MR * MC)).astype(jnp.bfloat16)
    return np.cos(row).astype(np.float32), np.sin(row).astype(np.float32), fwd, back


def fused(
    rd, x_ref, sw_ref, pw_ref, cw_ref, cos_ref, sin_ref, fwd_ref, back_ref, out_ref,
    v, kmat, x1, x2, rb, bsend, brecv, asend, arecv, gat, spec_out,
    h_send, h_recv, c_send, c_recv, a_send, a_recv, g_send, g_recv, f_send, f_recv,
):
    f32, bf16 = jnp.float32, jnp.bfloat16
    rows_here, _, cols_here = x_ref.shape
    wide = cols_here + PAD
    total_rows = rows_here + 2 * HALO
    owned = sw_ref.shape[1] // CH
    per_dest = owned // MC
    row_count = rows_here * rd
    norm = 1.0 / math.sqrt(row_count * cols_here * 2)
    r = lax.axis_index("rows")
    c = lax.axis_index("cols")
    sib = 1 - c
    row_at = lambda o: lax.rem(r + o + rd, rd)
    up, down = row_at(-1), row_at(1)

    def to(row, col):
        return {"rows": row, "cols": col}

    def remote(src, dst, ss, rs, row, col):
        return pltpu.make_async_remote_copy(
            src_ref=src, dst_ref=dst, send_sem=ss, recv_sem=rs,
            device_id=to(row, col), device_id_type=pl.DeviceIdType.MESH,
        )

    barrier = pltpu.get_barrier_semaphore()
    peers = [(row_at(o), c) for o in range(1, rd)] + [(r, sib), (up, sib), (down, sib)]
    for row, col in peers:
        pl.semaphore_signal(
            barrier, inc=1, device_id=to(row, col), device_id_type=pl.DeviceIdType.MESH
        )
    v[0, HALO:HALO + rows_here, :, 0:cols_here] = x_ref[...]
    pl.semaphore_wait(barrier, len(peers))

    edge = pl.multiple_of(sib * (cols_here - PAD), PAD)

    def halo_copies(l):
        vl = v.at[l]
        top, bottom = pl.ds(HALO, HALO), pl.ds(rows_here, HALO)
        own = pl.ds(HALO, rows_here)
        first_rows, last_rows = pl.ds(0, HALO), pl.ds(HALO + rows_here, HALO)
        body, rim, src_rim = pl.ds(0, cols_here), pl.ds(cols_here, PAD), pl.ds(edge, PAD)
        every = pl.ds(0, CH)
        plan = [
            (own, src_rim, own, rim, r, sib),
            (top, body, last_rows, body, up, c),
            (bottom, body, first_rows, body, down, c),
            (top, src_rim, last_rows, rim, up, sib),
            (bottom, src_rim, first_rows, rim, down, sib),
        ]
        return [
            remote(vl.at[sr, every, sc], vl.at[dr, every, dc], h_send.at[l, n], h_recv.at[l, n], row, col)
            for n, (sr, sc, dr, dc, row, col) in enumerate(plan)
        ]

    lane = lax.broadcasted_iota(jnp.int32, (1, wide), 1)
    mid = cols_here + PAD // 2
    low_side = (lane < mid).astype(f32)
    high_side = ((lane < cols_here) | (lane >= mid)).astype(f32)
    cf = c.astype(f32)
    lane_mask = low_side * (1.0 - cf) + high_side * cf
    sign = jnp.where(lax.broadcasted_iota(jnp.int32, (1, 2 * CH), 1) < CH, -1.0, 1.0).astype(f32)

    def mask_of(t):
        row = r * rows_here + t - HALO
        inside = jnp.where((row >= 0) & (row < row_count), 1.0, 0.0).astype(f32)
        return lane_mask * inside

    def stack(value):
        return jnp.concatenate(
            [pltpu.roll(value, 1, 1), value, pltpu.roll(value, wide - 1, 1)], 0
        ).astype(bf16)

    def build_weights(l):
        point = pw_ref[l].astype(f32).T
        none = jnp.zeros((CH, CH), f32)
        for s in range(3):
            for i in range(3):
                parts = [cw_ref[l, s, i, j].astype(f32) for j in range(3)]
                parts.append(point if (s == 2 and i == 1) else none)
                kmat[s, i * CH:(i + 1) * CH, :] = jnp.concatenate(parts, 1).astype(bf16)

    def summed(t):
        return rb[t - 1, 0:CH] + rb[t, CH:2 * CH] + rb[t + 1, 2 * CH:3 * CH]

    def conv_first(l):
        def one(t, carry):
            value = v[l, t].astype(f32) * mask_of(t)
            rb[t] = dot(kmat[0, :, 0:3 * CH], stack(value))
            return carry
        lax.fori_loop(0, total_rows, one, 0)
        def fin(t, carry):
            x1[t] = stack(gelu(summed(t)) * mask_of(t))
            return carry
        lax.fori_loop(1, total_rows - 1, fin, 0)

    def conv_second(l):
        def one(t, carry):
            rb[t] = dot(kmat[1, :, 0:3 * CH], x1[t])
            return carry
        lax.fori_loop(1, total_rows - 1, one, 0)
        def fin(t, carry):
            x2[t, 0:3 * CH] = stack(gelu(summed(t)) * mask_of(t))
            x2[t, 3 * CH:4 * CH] = v[l, t]
            return carry
        lax.fori_loop(2, total_rows - 2, fin, 0)

    def conv_third():
        def one(t, carry):
            rb[t] = dot(kmat[2], x2[t])
            return carry
        lax.fori_loop(2, total_rows - 2, one, 0)

    def row_block(us, ws, dest):
        parts = []
        for q in range(per_dest):
            k1 = (dest * 2 + c) * per_dest + q
            total = None
            for x in range(rows_here):
                at = r * rows_here + x
                term = cos_ref[k1, at] * us[x] + sin_ref[k1, at] * ws[x]
                total = term if total is None else total + term
            parts.append(total)
        return jnp.concatenate(parts, 0) if per_dest > 1 else parts[0]

    for l in range(LAYERS):
        halos = halo_copies(l)
        flat = v[l, HALO:HALO + rows_here, :, 0:cols_here].reshape(rows_here * CH, cols_here)
        bpart = lax.dot_general(
            fwd_ref[c], flat, (((1,), (1,)), ((), ())), preferred_element_type=f32
        )
        bsend[l] = bpart.astype(bf16)
        col_copy = remote(bsend.at[l], brecv.at[l], c_send.at[l], c_recv.at[l], r, sib)
        col_copy.start()
        for h in halos:
            h.start()
        build_weights(l)
        col_copy.wait_recv()
        cols_sum = bpart + brecv[l].astype(f32)
        us, ws = [], []
        for x in range(rows_here):
            re = cols_sum[0:MC, x * CH:(x + 1) * CH]
            im = -cols_sum[MC:2 * MC, x * CH:(x + 1) * CH]
            us.append(jnp.concatenate([re, im], 1))
            ws.append(jnp.concatenate([im, -re], 1))
        a_copies = []
        for o in range(1, rd):
            dest = row_at(o)
            asend[l, o] = row_block(us, ws, dest).astype(bf16)
            cp = remote(asend.at[l, o], arecv.at[l, o], a_send.at[l, o], a_recv.at[l, o], dest, c)
            cp.start()
            a_copies.append(cp)
        own_spec = row_block(us, ws, r)
        for h in halos:
            h.wait_recv()
        conv_first(l)
        for cp in a_copies:
            cp.wait_recv()
        spec = own_spec
        for o in range(1, rd):
            spec = spec + arecv[l, o].astype(f32)
        spec = spec * norm
        turned = pltpu.roll(spec, CH, 1)
        is_re = lax.broadcasted_iota(jnp.int32, (owned, 2 * CH), 1) < CH
        both = jnp.concatenate([jnp.where(is_re, spec, turned), jnp.where(is_re, turned, spec)], 0)
        mode_of_row = lax.rem(lax.broadcasted_iota(jnp.int32, (2 * owned, 2 * CH), 0), owned)
        half = lax.broadcasted_iota(jnp.int32, (2 * owned, 2 * CH), 1) // CH
        blocks = [
            jnp.where(mode_of_row == 2 * t + half, both, 0.0).astype(bf16) for t in range(owned // 2)
        ]
        mixed = dot(jnp.concatenate(blocks, 1), sw_ref[l])
        mixed = mixed[0:owned] + sign * pltpu.roll(mixed[owned:2 * owned], CH, 1)
        me = r * 2 + c
        gat[l, me] = mixed.astype(bf16)
        g_copies = []
        for o in range(1, rd):
            cp = remote(gat.at[l, me], gat.at[l, me], g_send.at[l, o], g_recv.at[l, o], row_at(o), c)
            cp.start()
            g_copies.append(cp)
        f_copies = [remote(gat.at[l, me], gat.at[l, me], f_send.at[l, 0], f_recv.at[l, 0], r, sib)]
        f_copies[0].start()
        conv_second(l)
        for o in range(1, rd):
            src = row_at(-o) * 2 + c
            remote(gat.at[l, src], gat.at[l, src], g_send.at[l, o], g_recv.at[l, o], row_at(o), c).wait_recv()
            cp = remote(gat.at[l, src], gat.at[l, src], f_send.at[l, o], f_recv.at[l, o], r, sib)
            cp.start()
            f_copies.append(cp)
        conv_third()

        sums = [None] * (2 * rows_here)

        def absorb(device):
            for q in range(per_dest):
                k1 = device * per_dest + q
                g = gat[l, device, q * MC:(q + 1) * MC].astype(f32)
                for x in range(rows_here):
                    at = r * rows_here + x
                    for n, tab in ((x, cos_ref), (rows_here + x, sin_ref)):
                        term = tab[k1, at] * g
                        sums[n] = term if sums[n] is None else sums[n] + term

        for o in range(rd):
            absorb(row_at(-o) * 2 + c)
        for o in range(rd):
            src = row_at(-o) * 2 + sib
            remote(gat.at[l, src], gat.at[l, src], f_send.at[l, o], f_recv.at[l, o], r, sib).wait_recv()
            absorb(src)
        backs = [sums[x] + sign * pltpu.roll(sums[rows_here + x], CH, 1) for x in range(rows_here)]
        backs = jnp.concatenate(
            [
                jnp.concatenate([b[:, 0:CH] for b in backs], 1),
                jnp.concatenate([b[:, CH:2 * CH] for b in backs], 1),
            ],
            0,
        )
        spec_out[...] = dot(backs.T.astype(bf16), back_ref[c])
        for x in range(rows_here):
            t = HALO + x
            result = gelu(
                spec_out[x * CH:(x + 1) * CH]
                + rb[t - 1, 0:CH, 0:cols_here]
                + rb[t, CH:2 * CH, 0:cols_here]
                + rb[t + 1, 2 * CH:3 * CH, 0:cols_here]
            ).astype(bf16)
            if l + 1 < LAYERS:
                v[l + 1, t, :, 0:cols_here] = result
            else:
                out_ref[x] = result
        for cp in [col_copy] + halos + a_copies + g_copies + f_copies:
            cp.wait_send()


def fused_shards(plume_field, spectral_weight, point_weight, conv_weight):
    _, rows_here, cols_here = plume_field.shape
    rd, cd = lax.axis_size("rows"), lax.axis_size("cols")
    owned = spectral_weight.shape[1]
    cos_t, sin_t, fwd, back = tables(rows_here * rd, cols_here * cd, cd)
    wide, total_rows = cols_here + PAD, rows_here + 2 * HALO
    f32, bf16 = jnp.float32, jnp.bfloat16
    vm = pl.BlockSpec(memory_space=pltpu.VMEM)
    sm = pl.BlockSpec(memory_space=pltpu.SMEM)
    dma = pltpu.SemaphoreType.DMA
    out = pl.pallas_call(
        functools.partial(fused, rd),
        out_shape=jax.ShapeDtypeStruct((rows_here, CH, cols_here), bf16),
        in_specs=[vm, vm, vm, vm, sm, sm, vm, vm],
        out_specs=vm,
        scratch_shapes=[
            pltpu.VMEM((LAYERS, total_rows, CH, wide), bf16),
            pltpu.VMEM((3, 3 * CH, 4 * CH), bf16),
            pltpu.VMEM((total_rows, 3 * CH, wide), bf16),
            pltpu.VMEM((total_rows, 4 * CH, wide), bf16),
            pltpu.VMEM((total_rows, 3 * CH, wide), f32),
            pltpu.VMEM((LAYERS, 2 * MC, rows_here * CH), bf16),
            pltpu.VMEM((LAYERS, 2 * MC, rows_here * CH), bf16),
            pltpu.VMEM((LAYERS, rd, owned, 2 * CH), bf16),
            pltpu.VMEM((LAYERS, rd, owned, 2 * CH), bf16),
            pltpu.VMEM((LAYERS, rd * cd, owned, 2 * CH), bf16),
            pltpu.VMEM((rows_here * CH, cols_here), f32),
            dma((LAYERS, 5)), dma((LAYERS, 5)),
            dma((LAYERS,)), dma((LAYERS,)),
            dma((LAYERS, rd)), dma((LAYERS, rd)),
            dma((LAYERS, rd)), dma((LAYERS, rd)),
            dma((LAYERS, rd)), dma((LAYERS, rd)),
        ],
        compiler_params=pltpu.CompilerParams(
            collective_id=0, has_side_effects=True, vmem_limit_bytes=48 * 1024 * 1024
        ),
    )(
        plume_field.transpose(1, 0, 2),
        spectral_weight.reshape(LAYERS, owned * CH, 2 * CH),
        point_weight,
        conv_weight.transpose(0, 1, 4, 5, 2, 3),
        cos_t, sin_t, fwd, back,
    )
    return out.transpose(1, 0, 2)


def routed(plume_field, spectral_weight, point_weight, conv_weight):
    _, rows_here, cols_here = plume_field.shape
    rd, cd = lax.axis_size("rows"), lax.axis_size("cols")
    owned = spectral_weight.shape[1]
    fits = (
        cd == 2 and 4 <= rd <= 16 and HALO <= rows_here <= 8
        and cols_here % PAD == 0 and cols_here <= 1024 and owned % MC == 0
    )
    return (fused_shards if fits else shards)(plume_field, spectral_weight, point_weight, conv_weight)


def solution(mesh):
    in_specs = (
        P(None, ("groups", "rows"), "cols"),
        P(None, ("rows", "cols"), None, None),
        P(),
        P(),
    )
    out_specs = P(None, ("groups", "rows"), "cols")
    return jax.shard_map(routed, mesh=mesh, in_specs=in_specs, out_specs=out_specs, check_vma=False)
```

```python
import math

import functools

import jax
import jax.numpy as jnp
import numpy as np
from jax import lax
from jax.experimental import pallas as pl
from jax.experimental.pallas import tpu as pltpu
from jax.sharding import PartitionSpec as P

CH = 64
MR = 32
MC = 32
LAYERS = 2


def with_halo(cells, sides, width):
    for axis, dim in sides:
        count = lax.axis_size(axis)
        ends = count - 1
        head = lax.slice_in_dim(cells, 0, width, axis=dim)
        tail = lax.slice_in_dim(cells, cells.shape[dim] - width, cells.shape[dim], axis=dim)
        cells = jnp.concatenate(
            [
                lax.ppermute(tail, axis, [(i, (i + 1) % count) for i in range(ends)]),
                cells,
                lax.ppermute(head, axis, [((i + 1) % count, i) for i in range(ends)]),
            ],
            axis=dim,
        )
    return cells


def angles(frequencies, positions, extent):
    product = frequencies[:, None] * positions[None, :] % extent
    return 2.0 * math.pi / extent * product.astype(jnp.float32)


def row_frequencies(extent):
    wave_index = jnp.arange(MR, dtype=jnp.int32)
    return jnp.where(wave_index < MR // 2, wave_index, extent - MR + wave_index)


def contract(form, left, right):
    return jnp.einsum(form, left, right, precision=lax.Precision.HIGHEST)


def convolve_valid(padded, kernel):
    result = lax.conv_general_dilated(
        padded[None],
        kernel,
        (1, 1),
        "VALID",
        dimension_numbers=("NCHW", "OIHW", "NCHW"),
        preferred_element_type=jnp.float32,
    )
    return result[0]


def rim_once(values):
    return with_halo(values, (("rows", 1), ("cols", 2)), 1)


def shards(plume_field, spectral_weight, point_weight, conv_weight):
    rows_here, cols_here = (plume_field.shape[1], plume_field.shape[2])
    row_devices, col_devices = (lax.axis_size("rows"), lax.axis_size("cols"))
    row_count, col_count = (rows_here * row_devices, cols_here * col_devices)
    row_start = lax.axis_index("rows") * rows_here
    col_start = lax.axis_index("cols") * cols_here
    row_positions = row_start + jnp.arange(rows_here, dtype=jnp.int32)
    col_positions = col_start + jnp.arange(cols_here, dtype=jnp.int32)
    row_theta = angles(row_frequencies(row_count), row_positions, row_count)
    col_theta = angles(jnp.arange(MC, dtype=jnp.int32), col_positions, col_count)
    cos_rows, sin_rows = (jnp.cos(row_theta), jnp.sin(row_theta))
    all_theta = angles(
        row_frequencies(row_count), jnp.arange(row_count, dtype=jnp.int32), row_count
    )
    cos_every, sin_every = (jnp.cos(all_theta), jnp.sin(all_theta))
    forward_table = jnp.concatenate([jnp.cos(col_theta), jnp.sin(col_theta)], 0).T.astype(
        jnp.bfloat16
    )
    back_table = jnp.concatenate([jnp.cos(col_theta), -jnp.sin(col_theta)], 0)
    norm_factor = 1.0 / math.sqrt(row_count * col_count)
    owned_count = MR * MC // (row_devices * col_devices)
    block_count = MR * MC // row_devices
    block_width = min(block_count, MC)
    block_depth = max(block_count // MC, 1)
    spread = MC // block_width
    pairs_here = block_width * CH // row_devices
    for layer_index in range(LAYERS):
        partial_value = jnp.einsum(
            "cxy,yk->cxk", plume_field, forward_table, preferred_element_type=jnp.float32
        )
        banded = lax.psum(partial_value.astype(jnp.bfloat16), "cols").astype(jnp.float32)
        pencil = banded.reshape(CH, rows_here, 2, spread, block_width).transpose(4, 0, 2, 3, 1)
        pencil = pencil.reshape(block_width * CH, 2, spread, rows_here)
        columns = lax.all_to_all(
            pencil.astype(jnp.bfloat16), "rows", split_axis=0, concat_axis=3, tiled=True
        ).astype(pencil.dtype)
        part_re, part_im = (columns[:, 0], -columns[:, 1])
        four_re = contract("kx,qvx->qvk", cos_every, part_re) + contract(
            "kx,qvx->qvk", sin_every, part_im
        )
        four_im = contract("kx,qvx->qvk", cos_every, part_im) - contract(
            "kx,qvx->qvk", sin_every, part_re
        )
        pencil_spec = jnp.stack([four_re, four_im], 1) * norm_factor
        outgoing = pencil_spec.reshape(
            pairs_here, 2, spread, MR // block_depth, block_depth
        ).transpose(3, 2, 0, 1, 4)
        outgoing = outgoing.reshape(row_devices, pairs_here, 2, block_depth)
        arrived = lax.all_to_all(outgoing, "rows", split_axis=0, concat_axis=0, tiled=True)
        block_spec = (
            arrived.reshape(block_width, CH, 2, block_depth)
            .transpose(3, 0, 2, 1)
            .reshape(block_count, 2 * CH)
        )
        owned_spectrum = lax.dynamic_slice_in_dim(
            block_spec, lax.axis_index("cols") * owned_count, owned_count, 0
        )
        rounded = owned_spectrum.astype(jnp.bfloat16).astype(jnp.float32)
        weight_wide = spectral_weight[layer_index].astype(jnp.float32)
        from_re = contract("mc,mcd->md", rounded[:, :CH], weight_wide)
        from_im = contract("mc,mcd->md", rounded[:, CH:], weight_wide)
        owned_mixed = jnp.concatenate(
            [from_re[:, :CH] - from_im[:, CH:], from_re[:, CH:] + from_im[:, :CH]], -1
        ).astype(jnp.bfloat16)
        every_mode = lax.all_gather(owned_mixed, ("rows", "cols"), axis=0, tiled=True)
        every_mode = every_mode.astype(jnp.float32).reshape(MR, MC, 2 * CH)
        mode_re, mode_im = (every_mode[..., :CH], every_mode[..., CH:])
        back_re = contract("kx,kjc->jxc", cos_rows, mode_re) - contract(
            "kx,kjc->jxc", sin_rows, mode_im
        )
        back_im = contract("kx,kjc->jxc", sin_rows, mode_re) + contract(
            "kx,kjc->jxc", cos_rows, mode_im
        )
        stacked = jnp.concatenate([back_re, back_im], 0)
        spectral_part = contract("jxc,jy->cxy", stacked, back_table) / math.sqrt(MR * MC)
        point_part = jnp.einsum(
            "co,cxy->oxy",
            point_weight[layer_index],
            plume_field,
            preferred_element_type=jnp.float32,
        )
        kernels = conv_weight[layer_index]
        first = jax.nn.gelu(convolve_valid(rim_once(plume_field), kernels[0])).astype(jnp.bfloat16)
        second = jax.nn.gelu(convolve_valid(rim_once(first), kernels[1])).astype(jnp.bfloat16)
        branch_out = convolve_valid(rim_once(second), kernels[2])
        plume_field = jax.nn.gelu(spectral_part + point_part + branch_out).astype(jnp.bfloat16)
    return plume_field


HALO = 3
EARLY = False
PAD = 128


def gelu(z):
    return 0.5 * z * (1.0 + jnp.tanh(math.sqrt(2.0 / math.pi) * (z + 0.044715 * z * z * z)))


def dot(a, b):
    return jnp.dot(a, b, preferred_element_type=jnp.float32)


def tables(row_count, col_count, col_devices):
    k = np.arange(MR)
    f1 = np.where(k < MR // 2, k, row_count - MR + k)
    row = 2.0 * math.pi / row_count * (f1[:, None] * np.arange(row_count)[None] % row_count)
    col = 2.0 * math.pi / col_count * (np.arange(MC)[:, None] * np.arange(col_count)[None] % col_count)
    split = lambda t: t.reshape(2 * MC, col_devices, -1).transpose(1, 0, 2)
    fwd = split(np.concatenate([np.cos(col), np.sin(col)], 0)).astype(jnp.bfloat16)
    back = split(np.concatenate([np.cos(col), -np.sin(col)], 0) / math.sqrt(MR * MC)).astype(jnp.bfloat16)
    trig = np.concatenate([np.cos(row), np.sin(row)], 0).astype(np.float32)
    trig = np.pad(trig, ((0, 0), (0, -row_count % PAD)))
    return trig, fwd, back


def fused(
    rd, x_ref, sw_hbm, pw_hbm, cw_hbm, trig_hbm, fwd_hbm, back_hbm, out_ref,
    sw_ref, pw_ref, cw_ref, trig, fwd_ref, back_ref, l_sem,
    v, kmat, x1, x2, rb, bsend, brecv, asend, arecv, gat, spec_out,
    h_send, h_recv, c_send, c_recv, a_send, a_recv, g_send, g_recv, f_send, f_recv,
):
    f32, bf16 = jnp.float32, jnp.bfloat16
    rows_here, _, cols_here = x_ref.shape
    wide = cols_here + PAD
    total_rows = rows_here + 2 * HALO
    owned = sw_hbm.shape[1] // CH
    per_dest = owned // MC
    row_count = rows_here * rd
    norm = 1.0 / math.sqrt(row_count * cols_here * 2)
    r = lax.axis_index("rows")
    c = lax.axis_index("cols")
    sib = 1 - c
    row_at = lambda o: lax.rem(r + o + rd, rd)
    up, down = row_at(-1), row_at(1)

    def to(row, col):
        return {"rows": row, "cols": col}

    def remote(src, dst, ss, rs, row, col):
        return pltpu.make_async_remote_copy(
            src_ref=src, dst_ref=dst, send_sem=ss, recv_sem=rs,
            device_id=to(row, col), device_id_type=pl.DeviceIdType.MESH,
        )

    barrier = pltpu.get_barrier_semaphore()
    peers = [(row_at(o), c) for o in range(1, rd)] + [(r, sib)]
    for row, col in peers:
        pl.semaphore_signal(
            barrier, inc=1, device_id=to(row, col), device_id_type=pl.DeviceIdType.MESH
        )
    loads = [
        pltpu.make_async_copy(src, dst, l_sem.at[n])
        for n, (src, dst) in enumerate(
            (
                (fwd_hbm.at[c], fwd_ref), (cw_hbm, cw_ref), (pw_hbm, pw_ref),
                (trig_hbm, trig), (sw_hbm, sw_ref), (back_hbm.at[c], back_ref),
            )
        )
    ]
    for load in loads:
        load.start()
    v[0, HALO:HALO + rows_here, :, 0:cols_here] = x_ref[...]

    @pl.when(r == 0)
    def _():
        v[:, 0:HALO, :, 0:cols_here] = jnp.zeros((LAYERS, HALO, CH, cols_here), bf16)

    @pl.when(r == rd - 1)
    def _():
        v[:, HALO + rows_here:, :, 0:cols_here] = jnp.zeros((LAYERS, HALO, CH, cols_here), bf16)

    edge = pl.multiple_of(sib * (cols_here - PAD), PAD)

    def halo_copies(l):
        vl = v.at[l]
        top, bottom = pl.ds(HALO, HALO), pl.ds(rows_here, HALO)
        own = pl.ds(HALO, rows_here)
        first_rows, last_rows = pl.ds(0, HALO), pl.ds(HALO + rows_here, HALO)
        body, rim, src_rim = pl.ds(0, cols_here), pl.ds(cols_here, PAD), pl.ds(edge, PAD)
        every = pl.ds(0, CH)
        plan = [
            (top, body, last_rows, body, up, c),
            (bottom, body, first_rows, body, down, c),
            (own, src_rim, own, rim, r, sib),
            (first_rows, src_rim, first_rows, rim, r, sib),
            (last_rows, src_rim, last_rows, rim, r, sib),
        ]
        return [
            remote(vl.at[sr, every, sc], vl.at[dr, every, dc], h_send.at[l, n], h_recv.at[l, n], row, col)
            for n, (sr, sc, dr, dc, row, col) in enumerate(plan)
        ]

    has_up, has_down = r > 0, r < rd - 1

    lane = lax.broadcasted_iota(jnp.int32, (1, wide), 1)
    mid = cols_here + PAD // 2
    low_side = (lane < mid).astype(f32)
    high_side = ((lane < cols_here) | (lane >= mid)).astype(f32)
    cf = c.astype(f32)
    lane_mask = low_side * (1.0 - cf) + high_side * cf
    sign = jnp.where(lax.broadcasted_iota(jnp.int32, (1, 2 * CH), 1) < CH, -1.0, 1.0).astype(f32)

    def mask_of(t):
        row = r * rows_here + t - HALO
        inside = jnp.where((row >= 0) & (row < row_count), 1.0, 0.0).astype(f32)
        return lane_mask * inside

    def stack(value):
        return jnp.concatenate(
            [pltpu.roll(value, 1, 1), value, pltpu.roll(value, wide - 1, 1)], 0
        ).astype(bf16)

    def build_weights(l):
        point = pw_ref[l].astype(f32).T
        none = jnp.zeros((CH, CH), f32)
        for s in range(3):
            for i in range(3):
                parts = [cw_ref[l, s, i, j].astype(f32) for j in range(3)]
                parts.append(point if (s == 2 and i == 1) else none)
                kmat[s, i * CH:(i + 1) * CH, :] = jnp.concatenate(parts, 1).astype(bf16)

    def summed(t):
        return rb[t - 1, 0:CH] + rb[t, CH:2 * CH] + rb[t + 1, 2 * CH:3 * CH]

    def conv_rows(l, low, high):
        def one(t, carry):
            value = v[l, t].astype(f32) * mask_of(t)
            rb[t] = dot(kmat[0, :, 0:3 * CH], stack(value))
            return carry
        lax.fori_loop(low, high, one, 0)

    def conv_first():
        def fin(t, carry):
            x1[t] = stack(gelu(summed(t)) * mask_of(t))
            return carry
        lax.fori_loop(1, total_rows - 1, fin, 0)

    def conv_second(l):
        def one(t, carry):
            rb[t] = dot(kmat[1, :, 0:3 * CH], x1[t])
            return carry
        lax.fori_loop(1, total_rows - 1, one, 0)
        def fin(t, carry):
            x2[t, 0:3 * CH] = stack(gelu(summed(t)) * mask_of(t))
            x2[t, 3 * CH:4 * CH] = v[l, t]
            return carry
        lax.fori_loop(2, total_rows - 2, fin, 0)

    def conv_third():
        def one(t, carry):
            rb[t] = dot(kmat[2], x2[t])
            return carry
        lax.fori_loop(2, total_rows - 2, one, 0)

    def row_block(us, ws, dest):
        parts = []
        for q in range(per_dest):
            k1 = (dest * 2 + c) * per_dest + q
            total = None
            for x in range(rows_here):
                at = r * rows_here + x
                term = trig[k1, at] * us[x] + trig[MR + k1, at] * ws[x]
                total = term if total is None else total + term
            parts.append(total)
        return jnp.concatenate(parts, 0) if per_dest > 1 else parts[0]

    for l in range(LAYERS):
        halos = halo_copies(l)
        flat = v[l, HALO:HALO + rows_here, :, 0:cols_here].reshape(rows_here * CH, cols_here)
        if l == 0:
            loads[0].wait()
        bpart = lax.dot_general(
            fwd_ref[...], flat, (((1,), (1,)), ((), ())), preferred_element_type=f32
        )
        bsend[l] = bpart.astype(bf16)
        col_copy = remote(bsend.at[l], brecv.at[l], c_send.at[l], c_recv.at[l], r, sib)
        if l == 0:
            pl.semaphore_wait(barrier, len(peers))
        col_copy.start()
        halos[2].start()
        if EARLY:
            pl.when(has_up)(halos[0].start)
            pl.when(has_down)(halos[1].start)
        if l == 0:
            for load in loads[1:4]:
                load.wait()
        build_weights(l)
        col_copy.wait_recv()
        cols_sum = bpart + brecv[l].astype(f32)
        us, ws = [], []
        for x in range(rows_here):
            re = cols_sum[0:MC, x * CH:(x + 1) * CH]
            im = -cols_sum[MC:2 * MC, x * CH:(x + 1) * CH]
            us.append(jnp.concatenate([re, im], 1))
            ws.append(jnp.concatenate([im, -re], 1))
        a_copies = []
        for o in range(1, rd):
            dest = row_at(o)
            asend[l, o] = row_block(us, ws, dest).astype(bf16)
            cp = remote(asend.at[l, o], arecv.at[l, o], a_send.at[l, o], a_recv.at[l, o], dest, c)
            cp.start()
            a_copies.append(cp)
        if not EARLY:
            pl.when(has_up)(halos[0].start)
            pl.when(has_down)(halos[1].start)
        own_spec = row_block(us, ws, r)
        halos[2].wait_recv()
        conv_rows(l, HALO, HALO + rows_here)
        if l == 0:
            for load in loads[4:]:
                load.wait()
        for cp in a_copies:
            cp.wait_recv()
        spec = own_spec
        for o in range(1, rd):
            spec = spec + arecv[l, o].astype(f32)
        spec = spec * norm
        turned = pltpu.roll(spec, CH, 1)
        is_re = lax.broadcasted_iota(jnp.int32, (owned, 2 * CH), 1) < CH
        both = jnp.concatenate([jnp.where(is_re, spec, turned), jnp.where(is_re, turned, spec)], 0)
        mode_of_row = lax.rem(lax.broadcasted_iota(jnp.int32, (2 * owned, 2 * CH), 0), owned)
        half = lax.broadcasted_iota(jnp.int32, (2 * owned, 2 * CH), 1) // CH
        blocks = [
            jnp.where(mode_of_row == 2 * t + half, both, 0.0).astype(bf16) for t in range(owned // 2)
        ]
        mixed = dot(jnp.concatenate(blocks, 1), sw_ref[l])
        mixed = mixed[0:owned] + sign * pltpu.roll(mixed[owned:2 * owned], CH, 1)
        me = r * 2 + c
        gat[l, me] = mixed.astype(bf16)
        g_copies = []
        for o in range(1, rd):
            cp = remote(gat.at[l, me], gat.at[l, me], g_send.at[l, o], g_recv.at[l, o], row_at(o), c)
            cp.start()
            g_copies.append(cp)
        f_copies = [remote(gat.at[l, me], gat.at[l, me], f_send.at[l, 0], f_recv.at[l, 0], r, sib)]
        f_copies[0].start()
        pl.when(has_up)(halos[1].wait_recv)
        pl.when(has_down)(halos[0].wait_recv)
        for h in halos[3:]:
            h.start()
        for o in range(1, rd):
            src = row_at(-o) * 2 + c
            remote(gat.at[l, src], gat.at[l, src], g_send.at[l, o], g_recv.at[l, o], row_at(o), c).wait_recv()
            cp = remote(gat.at[l, src], gat.at[l, src], f_send.at[l, o], f_recv.at[l, o], r, sib)
            cp.start()
            f_copies.append(cp)
        for h in halos[3:]:
            h.wait_recv()
        conv_rows(l, 0, HALO)
        conv_rows(l, HALO + rows_here, total_rows)
        conv_first()
        conv_second(l)
        conv_third()

        sums = [None] * (2 * rows_here)

        def absorb(device):
            for q in range(per_dest):
                k1 = device * per_dest + q
                g = gat[l, device, q * MC:(q + 1) * MC].astype(f32)
                for x in range(rows_here):
                    at = r * rows_here + x
                    for n, base in ((x, 0), (rows_here + x, MR)):
                        term = trig[base + k1, at] * g
                        sums[n] = term if sums[n] is None else sums[n] + term

        for o in range(rd):
            absorb(row_at(-o) * 2 + c)
        for o in range(rd):
            src = row_at(-o) * 2 + sib
            remote(gat.at[l, src], gat.at[l, src], f_send.at[l, o], f_recv.at[l, o], r, sib).wait_recv()
            absorb(src)
        backs = [sums[x] + sign * pltpu.roll(sums[rows_here + x], CH, 1) for x in range(rows_here)]
        backs = jnp.concatenate(
            [
                jnp.concatenate([b[:, 0:CH] for b in backs], 1),
                jnp.concatenate([b[:, CH:2 * CH] for b in backs], 1),
            ],
            0,
        )
        spec_out[...] = dot(backs.T.astype(bf16), back_ref[...])
        for x in range(rows_here):
            t = HALO + x
            result = gelu(
                spec_out[x * CH:(x + 1) * CH]
                + rb[t - 1, 0:CH, 0:cols_here]
                + rb[t, CH:2 * CH, 0:cols_here]
                + rb[t + 1, 2 * CH:3 * CH, 0:cols_here]
            ).astype(bf16)
            if l + 1 < LAYERS:
                v[l + 1, t, :, 0:cols_here] = result
            else:
                out_ref[x] = result
        pl.when(has_up)(halos[0].wait_send)
        pl.when(has_down)(halos[1].wait_send)
        for cp in [col_copy] + halos[2:] + a_copies + g_copies + f_copies:
            cp.wait_send()


def fused_shards(plume_field, spectral_weight, point_weight, conv_weight):
    _, rows_here, cols_here = plume_field.shape
    rd, cd = lax.axis_size("rows"), lax.axis_size("cols")
    owned = spectral_weight.shape[1]
    trig, fwd, back = tables(rows_here * rd, cols_here * cd, cd)
    wide, total_rows = cols_here + PAD, rows_here + 2 * HALO
    f32, bf16 = jnp.float32, jnp.bfloat16
    vm = pl.BlockSpec(memory_space=pltpu.VMEM)
    hbm = pl.BlockSpec(memory_space=pltpu.HBM)
    dma = pltpu.SemaphoreType.DMA
    out = pl.pallas_call(
        functools.partial(fused, rd),
        out_shape=jax.ShapeDtypeStruct((rows_here, CH, cols_here), bf16),
        in_specs=[vm] + [hbm] * 6,
        out_specs=vm,
        scratch_shapes=[
            pltpu.VMEM((LAYERS, owned * CH, 2 * CH), bf16),
            pltpu.VMEM(point_weight.shape, bf16),
            pltpu.VMEM((LAYERS, 3, 3, 3, CH, CH), bf16),
            pltpu.SMEM((2 * MR, PAD * (-(-rows_here * rd // PAD))), f32),
            pltpu.VMEM((2 * MC, cols_here), bf16),
            pltpu.VMEM((2 * MC, cols_here), bf16),
            dma((6,)),
            pltpu.VMEM((LAYERS, total_rows, CH, wide), bf16),
            pltpu.VMEM((3, 3 * CH, 4 * CH), bf16),
            pltpu.VMEM((total_rows, 3 * CH, wide), bf16),
            pltpu.VMEM((total_rows, 4 * CH, wide), bf16),
            pltpu.VMEM((total_rows, 3 * CH, wide), f32),
            pltpu.VMEM((LAYERS, 2 * MC, rows_here * CH), bf16),
            pltpu.VMEM((LAYERS, 2 * MC, rows_here * CH), bf16),
            pltpu.VMEM((LAYERS, rd, owned, 2 * CH), bf16),
            pltpu.VMEM((LAYERS, rd, owned, 2 * CH), bf16),
            pltpu.VMEM((LAYERS, rd * cd, owned, 2 * CH), bf16),
            pltpu.VMEM((rows_here * CH, cols_here), f32),
            dma((LAYERS, 5)), dma((LAYERS, 5)),
            dma((LAYERS,)), dma((LAYERS,)),
            dma((LAYERS, rd)), dma((LAYERS, rd)),
            dma((LAYERS, rd)), dma((LAYERS, rd)),
            dma((LAYERS, rd)), dma((LAYERS, rd)),
        ],
        compiler_params=pltpu.CompilerParams(
            collective_id=0, has_side_effects=True, vmem_limit_bytes=63 * 1024 * 1024
        ),
    )(
        plume_field.transpose(1, 0, 2),
        spectral_weight.reshape(LAYERS, owned * CH, 2 * CH),
        point_weight,
        conv_weight.transpose(0, 1, 4, 5, 2, 3),
        trig, fwd, back,
    )
    return out.transpose(1, 0, 2)


def routed(plume_field, spectral_weight, point_weight, conv_weight):
    _, rows_here, cols_here = plume_field.shape
    rd, cd = lax.axis_size("rows"), lax.axis_size("cols")
    owned = spectral_weight.shape[1]
    fits = (
        cd == 2 and 4 <= rd <= 16 and HALO <= rows_here <= 8
        and cols_here % PAD == 0 and cols_here <= 1024 and owned % MC == 0
    )
    return (fused_shards if fits else shards)(plume_field, spectral_weight, point_weight, conv_weight)


def solution(mesh):
    in_specs = (
        P(None, ("groups", "rows"), "cols"),
        P(None, ("rows", "cols"), None, None),
        P(),
        P(),
    )
    out_specs = P(None, ("groups", "rows"), "cols")
    return jax.shard_map(routed, mesh=mesh, in_specs=in_specs, out_specs=out_specs, check_vma=False)
```

```python
import math

import functools

import jax
import jax.numpy as jnp
import numpy as np
from jax import lax
from jax.experimental import pallas as pl
from jax.experimental.pallas import tpu as pltpu
from jax.sharding import PartitionSpec as P

CH = 64
MR = 32
MC = 32
LAYERS = 2


def with_halo(cells, sides, width):
    for axis, dim in sides:
        count = lax.axis_size(axis)
        ends = count - 1
        head = lax.slice_in_dim(cells, 0, width, axis=dim)
        tail = lax.slice_in_dim(cells, cells.shape[dim] - width, cells.shape[dim], axis=dim)
        cells = jnp.concatenate(
            [
                lax.ppermute(tail, axis, [(i, (i + 1) % count) for i in range(ends)]),
                cells,
                lax.ppermute(head, axis, [((i + 1) % count, i) for i in range(ends)]),
            ],
            axis=dim,
        )
    return cells


def angles(frequencies, positions, extent):
    product = frequencies[:, None] * positions[None, :] % extent
    return 2.0 * math.pi / extent * product.astype(jnp.float32)


def row_frequencies(extent):
    wave_index = jnp.arange(MR, dtype=jnp.int32)
    return jnp.where(wave_index < MR // 2, wave_index, extent - MR + wave_index)


def contract(form, left, right):
    return jnp.einsum(form, left, right, precision=lax.Precision.HIGHEST)


def convolve_valid(padded, kernel):
    result = lax.conv_general_dilated(
        padded[None],
        kernel,
        (1, 1),
        "VALID",
        dimension_numbers=("NCHW", "OIHW", "NCHW"),
        preferred_element_type=jnp.float32,
    )
    return result[0]


def rim_once(values):
    return with_halo(values, (("rows", 1), ("cols", 2)), 1)


def shards(plume_field, spectral_weight, point_weight, conv_weight):
    rows_here, cols_here = (plume_field.shape[1], plume_field.shape[2])
    row_devices, col_devices = (lax.axis_size("rows"), lax.axis_size("cols"))
    row_count, col_count = (rows_here * row_devices, cols_here * col_devices)
    row_start = lax.axis_index("rows") * rows_here
    col_start = lax.axis_index("cols") * cols_here
    row_positions = row_start + jnp.arange(rows_here, dtype=jnp.int32)
    col_positions = col_start + jnp.arange(cols_here, dtype=jnp.int32)
    row_theta = angles(row_frequencies(row_count), row_positions, row_count)
    col_theta = angles(jnp.arange(MC, dtype=jnp.int32), col_positions, col_count)
    cos_rows, sin_rows = (jnp.cos(row_theta), jnp.sin(row_theta))
    all_theta = angles(
        row_frequencies(row_count), jnp.arange(row_count, dtype=jnp.int32), row_count
    )
    cos_every, sin_every = (jnp.cos(all_theta), jnp.sin(all_theta))
    forward_table = jnp.concatenate([jnp.cos(col_theta), jnp.sin(col_theta)], 0).T.astype(
        jnp.bfloat16
    )
    back_table = jnp.concatenate([jnp.cos(col_theta), -jnp.sin(col_theta)], 0)
    norm_factor = 1.0 / math.sqrt(row_count * col_count)
    owned_count = MR * MC // (row_devices * col_devices)
    block_count = MR * MC // row_devices
    block_width = min(block_count, MC)
    block_depth = max(block_count // MC, 1)
    spread = MC // block_width
    pairs_here = block_width * CH // row_devices
    for layer_index in range(LAYERS):
        partial_value = jnp.einsum(
            "cxy,yk->cxk", plume_field, forward_table, preferred_element_type=jnp.float32
        )
        banded = lax.psum(partial_value.astype(jnp.bfloat16), "cols").astype(jnp.float32)
        pencil = banded.reshape(CH, rows_here, 2, spread, block_width).transpose(4, 0, 2, 3, 1)
        pencil = pencil.reshape(block_width * CH, 2, spread, rows_here)
        columns = lax.all_to_all(
            pencil.astype(jnp.bfloat16), "rows", split_axis=0, concat_axis=3, tiled=True
        ).astype(pencil.dtype)
        part_re, part_im = (columns[:, 0], -columns[:, 1])
        four_re = contract("kx,qvx->qvk", cos_every, part_re) + contract(
            "kx,qvx->qvk", sin_every, part_im
        )
        four_im = contract("kx,qvx->qvk", cos_every, part_im) - contract(
            "kx,qvx->qvk", sin_every, part_re
        )
        pencil_spec = jnp.stack([four_re, four_im], 1) * norm_factor
        outgoing = pencil_spec.reshape(
            pairs_here, 2, spread, MR // block_depth, block_depth
        ).transpose(3, 2, 0, 1, 4)
        outgoing = outgoing.reshape(row_devices, pairs_here, 2, block_depth)
        arrived = lax.all_to_all(outgoing, "rows", split_axis=0, concat_axis=0, tiled=True)
        block_spec = (
            arrived.reshape(block_width, CH, 2, block_depth)
            .transpose(3, 0, 2, 1)
            .reshape(block_count, 2 * CH)
        )
        owned_spectrum = lax.dynamic_slice_in_dim(
            block_spec, lax.axis_index("cols") * owned_count, owned_count, 0
        )
        rounded = owned_spectrum.astype(jnp.bfloat16).astype(jnp.float32)
        weight_wide = spectral_weight[layer_index].astype(jnp.float32)
        from_re = contract("mc,mcd->md", rounded[:, :CH], weight_wide)
        from_im = contract("mc,mcd->md", rounded[:, CH:], weight_wide)
        owned_mixed = jnp.concatenate(
            [from_re[:, :CH] - from_im[:, CH:], from_re[:, CH:] + from_im[:, :CH]], -1
        ).astype(jnp.bfloat16)
        every_mode = lax.all_gather(owned_mixed, ("rows", "cols"), axis=0, tiled=True)
        every_mode = every_mode.astype(jnp.float32).reshape(MR, MC, 2 * CH)
        mode_re, mode_im = (every_mode[..., :CH], every_mode[..., CH:])
        back_re = contract("kx,kjc->jxc", cos_rows, mode_re) - contract(
            "kx,kjc->jxc", sin_rows, mode_im
        )
        back_im = contract("kx,kjc->jxc", sin_rows, mode_re) + contract(
            "kx,kjc->jxc", cos_rows, mode_im
        )
        stacked = jnp.concatenate([back_re, back_im], 0)
        spectral_part = contract("jxc,jy->cxy", stacked, back_table) / math.sqrt(MR * MC)
        point_part = jnp.einsum(
            "co,cxy->oxy",
            point_weight[layer_index],
            plume_field,
            preferred_element_type=jnp.float32,
        )
        kernels = conv_weight[layer_index]
        first = jax.nn.gelu(convolve_valid(rim_once(plume_field), kernels[0])).astype(jnp.bfloat16)
        second = jax.nn.gelu(convolve_valid(rim_once(first), kernels[1])).astype(jnp.bfloat16)
        branch_out = convolve_valid(rim_once(second), kernels[2])
        plume_field = jax.nn.gelu(spectral_part + point_part + branch_out).astype(jnp.bfloat16)
    return plume_field


HALO = 3
UNROLL = 2
PAD = 128


def gelu(z):
    return 0.5 * z * (1.0 + jnp.tanh(math.sqrt(2.0 / math.pi) * (z + 0.044715 * z * z * z)))


def dot(a, b):
    return jnp.dot(a, b, preferred_element_type=jnp.float32)


def tables(row_count, col_count, col_devices):
    k = np.arange(MR)
    f1 = np.where(k < MR // 2, k, row_count - MR + k)
    row = 2.0 * math.pi / row_count * (f1[:, None] * np.arange(row_count)[None] % row_count)
    col = 2.0 * math.pi / col_count * (np.arange(MC)[:, None] * np.arange(col_count)[None] % col_count)
    split = lambda t: t.reshape(2 * MC, col_devices, -1).transpose(1, 0, 2)
    fwd = split(np.concatenate([np.cos(col), np.sin(col)], 0)).astype(jnp.bfloat16)
    back = split(np.concatenate([np.cos(col), -np.sin(col)], 0) / math.sqrt(MR * MC)).astype(jnp.bfloat16)
    trig = np.concatenate([np.cos(row), np.sin(row)], 0).astype(np.float32)
    trig = np.pad(trig, ((0, 0), (0, -row_count % PAD)))
    return trig, fwd, back


def fused(
    rd, x_ref, sw_hbm, pw_hbm, cw_hbm, trig_hbm, fwd_hbm, back_hbm, out_ref,
    sw_ref, pw_ref, cw_ref, trig, fwd_ref, back_ref, l_sem,
    v, kmat, rb, rb2, bsend, brecv, asend, arecv, gat, spec_out,
    h_send, h_recv, c_send, c_recv, a_send, a_recv, g_send, g_recv, f_send, f_recv,
):
    f32, bf16 = jnp.float32, jnp.bfloat16
    rows_here, _, cols_here = x_ref.shape
    wide = cols_here + PAD
    total_rows = rows_here + 2 * HALO
    owned = sw_hbm.shape[1] // CH
    per_dest = owned // MC
    row_count = rows_here * rd
    norm = 1.0 / math.sqrt(row_count * cols_here * 2)
    r = lax.axis_index("rows")
    c = lax.axis_index("cols")
    sib = 1 - c
    row_at = lambda o: lax.rem(r + o + rd, rd)
    up, down = row_at(-1), row_at(1)

    def to(row, col):
        return {"rows": row, "cols": col}

    def remote(src, dst, ss, rs, row, col):
        return pltpu.make_async_remote_copy(
            src_ref=src, dst_ref=dst, send_sem=ss, recv_sem=rs,
            device_id=to(row, col), device_id_type=pl.DeviceIdType.MESH,
        )

    barrier = pltpu.get_barrier_semaphore()
    peers = [(row_at(o), c) for o in range(1, rd)] + [(r, sib)]
    for row, col in peers:
        pl.semaphore_signal(
            barrier, inc=1, device_id=to(row, col), device_id_type=pl.DeviceIdType.MESH
        )
    loads = [
        pltpu.make_async_copy(src, dst, l_sem.at[n])
        for n, (src, dst) in enumerate(
            (
                (fwd_hbm.at[c], fwd_ref), (cw_hbm, cw_ref), (pw_hbm, pw_ref),
                (trig_hbm, trig), (sw_hbm, sw_ref), (back_hbm.at[c], back_ref),
            )
        )
    ]
    for load in loads:
        load.start()
    v[0, HALO:HALO + rows_here, :, 0:cols_here] = x_ref[...]

    @pl.when(r == 0)
    def _():
        v[:, 0:HALO, :, 0:cols_here] = jnp.zeros((LAYERS, HALO, CH, cols_here), bf16)

    @pl.when(r == rd - 1)
    def _():
        v[:, HALO + rows_here:, :, 0:cols_here] = jnp.zeros((LAYERS, HALO, CH, cols_here), bf16)

    edge = pl.multiple_of(sib * (cols_here - PAD), PAD)

    def halo_copies(l):
        vl = v.at[l]
        top, bottom = pl.ds(HALO, HALO), pl.ds(rows_here, HALO)
        own = pl.ds(HALO, rows_here)
        first_rows, last_rows = pl.ds(0, HALO), pl.ds(HALO + rows_here, HALO)
        body, rim, src_rim = pl.ds(0, cols_here), pl.ds(cols_here, PAD), pl.ds(edge, PAD)
        every = pl.ds(0, CH)
        plan = [
            (top, body, last_rows, body, up, c),
            (bottom, body, first_rows, body, down, c),
            (own, src_rim, own, rim, r, sib),
            (first_rows, src_rim, first_rows, rim, r, sib),
            (last_rows, src_rim, last_rows, rim, r, sib),
        ]
        return [
            remote(vl.at[sr, every, sc], vl.at[dr, every, dc], h_send.at[l, n], h_recv.at[l, n], row, col)
            for n, (sr, sc, dr, dc, row, col) in enumerate(plan)
        ]

    has_up, has_down = r > 0, r < rd - 1

    lane = lax.broadcasted_iota(jnp.int32, (1, wide), 1)
    mid = cols_here + PAD // 2
    low_side = (lane < mid).astype(f32)
    high_side = ((lane < cols_here) | (lane >= mid)).astype(f32)
    cf = c.astype(f32)
    lane_mask = low_side * (1.0 - cf) + high_side * cf
    sign = jnp.where(lax.broadcasted_iota(jnp.int32, (1, 2 * CH), 1) < CH, -1.0, 1.0).astype(f32)

    def mask_of(t):
        row = r * rows_here + t - HALO
        inside = jnp.where((row >= 0) & (row < row_count), 1.0, 0.0).astype(f32)
        return lane_mask * inside

    def stack(value):
        return jnp.concatenate(
            [pltpu.roll(value, 1, 1), value, pltpu.roll(value, wide - 1, 1)], 0
        ).astype(bf16)

    def build_weights(l):
        point = pw_ref[l].astype(f32).T
        none = jnp.zeros((CH, CH), f32)
        for s in range(3):
            for i in range(3):
                parts = [cw_ref[l, s, i, j].astype(f32) for j in range(3)]
                parts.append(point if (s == 2 and i == 1) else none)
                kmat[s, i * CH:(i + 1) * CH, :] = jnp.concatenate(parts, 1).astype(bf16)

    def summed(rows, t):
        return rows[t - 1, 0:CH] + rows[t, CH:2 * CH] + rows[t + 1, 2 * CH:3 * CH]

    def conv_first(l, low, high):
        def one(t, carry):
            value = v[l, t].astype(f32) * mask_of(t)
            rb[t] = dot(kmat[0, :, 0:3 * CH], stack(value))
            return carry
        lax.fori_loop(low, high, one, 0, unroll=min(UNROLL, high - low))

    def conv_second(low, high):
        def one(t, carry):
            value = gelu(summed(rb, t)) * mask_of(t)
            rb2[t] = dot(kmat[1, :, 0:3 * CH], stack(value))
            return carry
        lax.fori_loop(low, high, one, 0, unroll=min(UNROLL, high - low))

    def conv_third(l):
        def one(t, carry):
            value = gelu(summed(rb2, t)) * mask_of(t)
            rb[t] = dot(kmat[2], jnp.concatenate([stack(value), v[l, t]], 0))
            return carry
        lax.fori_loop(2, total_rows - 2, one, 0, unroll=UNROLL)

    def row_block(us, ws, dest):
        parts = []
        for q in range(per_dest):
            k1 = (dest * 2 + c) * per_dest + q
            total = None
            for x in range(rows_here):
                at = r * rows_here + x
                term = trig[k1, at] * us[x] + trig[MR + k1, at] * ws[x]
                total = term if total is None else total + term
            parts.append(total)
        return jnp.concatenate(parts, 0) if per_dest > 1 else parts[0]

    for l in range(LAYERS):
        halos = halo_copies(l)
        flat = v[l, HALO:HALO + rows_here, :, 0:cols_here].reshape(rows_here * CH, cols_here)
        if l == 0:
            loads[0].wait()
        bpart = lax.dot_general(
            fwd_ref[...], flat, (((1,), (1,)), ((), ())), preferred_element_type=f32
        )
        bsend[l] = bpart.astype(bf16)
        col_copy = remote(bsend.at[l], brecv.at[l], c_send.at[l], c_recv.at[l], r, sib)
        if l == 0:
            pl.semaphore_wait(barrier, len(peers))
        col_copy.start()
        halos[2].start()
        if l == 0:
            for load in loads[1:4]:
                load.wait()
        build_weights(l)
        col_copy.wait_recv()
        cols_sum = bpart + brecv[l].astype(f32)
        us, ws = [], []
        for x in range(rows_here):
            re = cols_sum[0:MC, x * CH:(x + 1) * CH]
            im = -cols_sum[MC:2 * MC, x * CH:(x + 1) * CH]
            us.append(jnp.concatenate([re, im], 1))
            ws.append(jnp.concatenate([im, -re], 1))
        a_copies = []
        for o in range(1, rd):
            dest = row_at(o)
            asend[l, o] = row_block(us, ws, dest).astype(bf16)
            cp = remote(asend.at[l, o], arecv.at[l, o], a_send.at[l, o], a_recv.at[l, o], dest, c)
            cp.start()
            a_copies.append(cp)
        pl.when(has_up)(halos[0].start)
        pl.when(has_down)(halos[1].start)
        own_spec = row_block(us, ws, r)
        halos[2].wait_recv()
        conv_first(l, HALO, HALO + rows_here)
        conv_second(HALO + 1, HALO + rows_here - 1)
        if l == 0:
            for load in loads[4:]:
                load.wait()
        for cp in a_copies:
            cp.wait_recv()
        spec = own_spec
        for o in range(1, rd):
            spec = spec + arecv[l, o].astype(f32)
        spec = spec * norm
        turned = pltpu.roll(spec, CH, 1)
        is_re = lax.broadcasted_iota(jnp.int32, (owned, 2 * CH), 1) < CH
        both = jnp.concatenate([jnp.where(is_re, spec, turned), jnp.where(is_re, turned, spec)], 0)
        mode_of_row = lax.rem(lax.broadcasted_iota(jnp.int32, (2 * owned, 2 * CH), 0), owned)
        half = lax.broadcasted_iota(jnp.int32, (2 * owned, 2 * CH), 1) // CH
        blocks = [
            jnp.where(mode_of_row == 2 * t + half, both, 0.0).astype(bf16) for t in range(owned // 2)
        ]
        mixed = dot(jnp.concatenate(blocks, 1), sw_ref[l])
        mixed = mixed[0:owned] + sign * pltpu.roll(mixed[owned:2 * owned], CH, 1)
        me = r * 2 + c
        gat[l, me] = mixed.astype(bf16)
        g_copies = []
        for o in range(1, rd):
            cp = remote(gat.at[l, me], gat.at[l, me], g_send.at[l, o], g_recv.at[l, o], row_at(o), c)
            cp.start()
            g_copies.append(cp)
        f_copies = [remote(gat.at[l, me], gat.at[l, me], f_send.at[l, 0], f_recv.at[l, 0], r, sib)]
        f_copies[0].start()
        pl.when(has_up)(halos[1].wait_recv)
        pl.when(has_down)(halos[0].wait_recv)
        for h in halos[3:]:
            h.start()
        for h in halos[3:]:
            h.wait_recv()
        conv_first(l, 0, HALO)
        conv_first(l, HALO + rows_here, total_rows)
        conv_second(1, HALO + 1)
        conv_second(HALO + rows_here - 1, total_rows - 1)
        for o in range(1, rd):
            src = row_at(-o) * 2 + c
            remote(gat.at[l, src], gat.at[l, src], g_send.at[l, o], g_recv.at[l, o], row_at(o), c).wait_recv()
            cp = remote(gat.at[l, src], gat.at[l, src], f_send.at[l, o], f_recv.at[l, o], r, sib)
            cp.start()
            f_copies.append(cp)
        conv_third(l)

        sums = [None] * (2 * rows_here)

        def absorb(device):
            for q in range(per_dest):
                k1 = device * per_dest + q
                g = gat[l, device, q * MC:(q + 1) * MC].astype(f32)
                for x in range(rows_here):
                    at = r * rows_here + x
                    for n, base in ((x, 0), (rows_here + x, MR)):
                        term = trig[base + k1, at] * g
                        sums[n] = term if sums[n] is None else sums[n] + term

        for o in range(rd):
            absorb(row_at(-o) * 2 + c)
        for o in range(rd):
            src = row_at(-o) * 2 + sib
            remote(gat.at[l, src], gat.at[l, src], f_send.at[l, o], f_recv.at[l, o], r, sib).wait_recv()
            absorb(src)
        backs = [sums[x] + sign * pltpu.roll(sums[rows_here + x], CH, 1) for x in range(rows_here)]
        backs = jnp.concatenate(
            [
                jnp.concatenate([b[:, 0:CH] for b in backs], 1),
                jnp.concatenate([b[:, CH:2 * CH] for b in backs], 1),
            ],
            0,
        )
        spec_out[...] = dot(backs.T.astype(bf16), back_ref[...])
        for x in range(rows_here):
            t = HALO + x
            result = gelu(
                spec_out[x * CH:(x + 1) * CH]
                + rb[t - 1, 0:CH, 0:cols_here]
                + rb[t, CH:2 * CH, 0:cols_here]
                + rb[t + 1, 2 * CH:3 * CH, 0:cols_here]
            ).astype(bf16)
            if l + 1 < LAYERS:
                v[l + 1, t, :, 0:cols_here] = result
            else:
                out_ref[x] = result
        pl.when(has_up)(halos[0].wait_send)
        pl.when(has_down)(halos[1].wait_send)
        for cp in [col_copy] + halos[2:] + a_copies + g_copies + f_copies:
            cp.wait_send()


def fused_shards(plume_field, spectral_weight, point_weight, conv_weight):
    _, rows_here, cols_here = plume_field.shape
    rd, cd = lax.axis_size("rows"), lax.axis_size("cols")
    owned = spectral_weight.shape[1]
    trig, fwd, back = tables(rows_here * rd, cols_here * cd, cd)
    wide, total_rows = cols_here + PAD, rows_here + 2 * HALO
    f32, bf16 = jnp.float32, jnp.bfloat16
    vm = pl.BlockSpec(memory_space=pltpu.VMEM)
    hbm = pl.BlockSpec(memory_space=pltpu.HBM)
    dma = pltpu.SemaphoreType.DMA
    out = pl.pallas_call(
        functools.partial(fused, rd),
        out_shape=jax.ShapeDtypeStruct((rows_here, CH, cols_here), bf16),
        in_specs=[vm] + [hbm] * 6,
        out_specs=vm,
        scratch_shapes=[
            pltpu.VMEM((LAYERS, owned * CH, 2 * CH), bf16),
            pltpu.VMEM(point_weight.shape, bf16),
            pltpu.VMEM((LAYERS, 3, 3, 3, CH, CH), bf16),
            pltpu.SMEM((2 * MR, PAD * (-(-rows_here * rd // PAD))), f32),
            pltpu.VMEM((2 * MC, cols_here), bf16),
            pltpu.VMEM((2 * MC, cols_here), bf16),
            dma((6,)),
            pltpu.VMEM((LAYERS, total_rows, CH, wide), bf16),
            pltpu.VMEM((3, 3 * CH, 4 * CH), bf16),
            pltpu.VMEM((total_rows, 3 * CH, wide), f32),
            pltpu.VMEM((total_rows, 3 * CH, wide), f32),
            pltpu.VMEM((LAYERS, 2 * MC, rows_here * CH), bf16),
            pltpu.VMEM((LAYERS, 2 * MC, rows_here * CH), bf16),
            pltpu.VMEM((LAYERS, rd, owned, 2 * CH), bf16),
            pltpu.VMEM((LAYERS, rd, owned, 2 * CH), bf16),
            pltpu.VMEM((LAYERS, rd * cd, owned, 2 * CH), bf16),
            pltpu.VMEM((rows_here * CH, cols_here), f32),
            dma((LAYERS, 5)), dma((LAYERS, 5)),
            dma((LAYERS,)), dma((LAYERS,)),
            dma((LAYERS, rd)), dma((LAYERS, rd)),
            dma((LAYERS, rd)), dma((LAYERS, rd)),
            dma((LAYERS, rd)), dma((LAYERS, rd)),
        ],
        compiler_params=pltpu.CompilerParams(
            collective_id=0, has_side_effects=True, vmem_limit_bytes=63 * 1024 * 1024
        ),
    )(
        plume_field.transpose(1, 0, 2),
        spectral_weight.reshape(LAYERS, owned * CH, 2 * CH),
        point_weight,
        conv_weight.transpose(0, 1, 4, 5, 2, 3),
        trig, fwd, back,
    )
    return out.transpose(1, 0, 2)


def routed(plume_field, spectral_weight, point_weight, conv_weight):
    _, rows_here, cols_here = plume_field.shape
    rd, cd = lax.axis_size("rows"), lax.axis_size("cols")
    owned = spectral_weight.shape[1]
    fits = (
        cd == 2 and 4 <= rd <= 16 and HALO <= rows_here <= 8
        and cols_here % PAD == 0 and cols_here <= 1024 and owned % MC == 0
    )
    return (fused_shards if fits else shards)(plume_field, spectral_weight, point_weight, conv_weight)


def solution(mesh):
    in_specs = (
        P(None, ("groups", "rows"), "cols"),
        P(None, ("rows", "cols"), None, None),
        P(),
        P(),
    )
    out_specs = P(None, ("groups", "rows"), "cols")
    return jax.shard_map(routed, mesh=mesh, in_specs=in_specs, out_specs=out_specs, check_vma=False)
```
